32 devices in a mesh: store: 8 (over y, x, core), tp: 4 (over z).
Axes of the slice: x: 2, y: 2, z: 4, core: 2. Of those that a mesh axis runs over, the one named last changes fastest.
Arguments:
- queries: bfloat16 [8, 512, 4096], P('store', 'tp')
- suffix_keys: bfloat16 [8, 512, 512], P('store', 'tp'), may hold values from -6 to 6
- suffix_values: bfloat16 [8, 512, 512], P('store', 'tp'), may hold values from -6 to 6
- passage_keys: bfloat16 [8, 2048, 512], P(None, 'store')
- passage_values: bfloat16 [8, 2048, 512], P(None, 'store'), may hold values from -6 to 6
- cites: int32 [8, 2], replicated, may hold values from 0 to 7, all different within a row
- passage_row: int32 [8], replicated, may hold values from 0 to 7, each once
- suffix_len: int32 [8], replicated, may hold values from 1 to 512, as said below
Outputs:
- context: bfloat16 [8, 512, 4096], P('store', 'tp')
- decode_keys: bfloat16 [8, 512, 512], P('store', None, 'tp')
- decode_values: bfloat16 [8, 512, 512], P('store', None, 'tp')
The draws below stay inside these ranges and needn't reach their ends.
Inputs may be any that keep to these rules, and one draw needn't show every extreme that they name: Each request cites 2 different passages; every passage is cited by some request. `passage_row`: each store row holds exactly one passage id. `suffix_len`: some request has all 512 suffix tokens live.
All inputs are finite; a program needn't handle non-finite values.
Results may differ from the reference program's by a relative error of at most 0.0085.
Values may be sent and summed in bfloat16 or wider, within the bound.
A program may use at most 128 MiB of HBM per device.

```python
import jax
import jax.numpy as jnp
from jax import lax

HD = 128
HQ = 32
KVH = 4
PLEN = 2048
CITE = 2
SUF = 512
NREQ = 8
NPASS = 8


def draw_queries(key, part):
    key = jax.random.fold_in(key, 11)
    shape = (NREQ, SUF, HQ, HD)
    base = 2.5 * jax.random.truncated_normal(jax.random.fold_in(key, 1), -6.0, 6.0, shape, jnp.float32)
    return base.reshape(NREQ, SUF, HQ * HD).astype(jnp.bfloat16)


def draw_passage_keys(key, part):
    key = jax.random.fold_in(key, 12)
    shape = (NPASS, PLEN, KVH, HD)
    base = jax.random.truncated_normal(jax.random.fold_in(key, 1), -6.0, 6.0, shape, jnp.float32)
    return base.reshape(NPASS, PLEN, KVH * HD).astype(jnp.bfloat16)


def draw_suffix_len(key, part):
    key = jax.random.fold_in(key, 13)
    lengths = jax.random.randint(jax.random.fold_in(key, 1), (NREQ,), 1, SUF + 1)
    fullest = jax.random.randint(jax.random.fold_in(key, 2), (), 0, NREQ)
    return jnp.where(jnp.arange(NREQ) == fullest, SUF, lengths).astype(jnp.int32)


def steps_of(key, shape, split, least, high):
    def one(position, parts):
        heights = jax.random.uniform(jax.random.fold_in(jax.random.fold_in(key, 6), position), (parts,), jnp.float32, least / len(split), high / len(split))
        return jnp.repeat(jnp.exp(heights), shape[position] // parts).reshape((-1,) + (1,) * (len(shape) - position - 1))

    loudness = one(*split[0])
    for cut in split[1:]:
        loudness = loudness * one(*cut)
    return loudness


def different_ones(rng, rows, amount, top, lift):
    order = jax.random.permutation(jax.random.fold_in(rng, 1), amount)
    favour = order
    for power in range(3):
        favour = favour * favour // amount
    favour = favour * lift // amount
    chance = jax.random.randint(jax.random.fold_in(rng, 2), (rows, amount), 0, 4096) + favour
    fixed_rows = jax.random.permutation(jax.random.fold_in(rng, 3), rows)[jnp.arange(amount) % rows]
    chance = jnp.where(jnp.arange(rows)[:, None] == fixed_rows[None, :], 1 << 14, chance)
    merit = chance * amount + jnp.arange(amount)
    return lax.top_k(merit.astype(jnp.int32), top)[1].astype(jnp.int32)


def normal_values(rng, dims, width, limit, split=(), kind=jnp.bfloat16):
    array = width * jax.random.normal(rng, dims, jnp.float32)
    if split:
        array = array * steps_of(rng, dims, split, -0.22, 0.18)
    return jnp.clip(array, -limit, limit).astype(kind)


def setup_inputs(seed: int = 0) -> dict:
    key_of = jax.random.split(jax.random.key(seed), 9)
    queries = draw_queries(jax.random.fold_in(key_of[8], 71), 0)
    suffix_keys = normal_values(key_of[1], (NREQ, SUF, KVH * HD), 1.0, 6.0, ((0, 8), (1, 4)))
    suffix_values = normal_values(key_of[2], (NREQ, SUF, KVH * HD), 1.0, 6.0, ((0, 8), (1, 4)))
    passage_keys = draw_passage_keys(jax.random.fold_in(key_of[8], 71), 0)
    passage_values = normal_values(key_of[4], (NPASS, PLEN, KVH * HD), 1.0, 6.0, ((1, 8),))
    cites = different_ones(key_of[5], NREQ, NPASS, CITE, 4096)
    passage_row = jax.random.permutation(key_of[6], NPASS).astype(jnp.int32)
    suffix_len = draw_suffix_len(jax.random.fold_in(key_of[8], 71), 0)
    return {"queries": queries, "suffix_keys": suffix_keys, "suffix_values": suffix_values, "passage_keys": passage_keys, "passage_values": passage_values, "cites": cites, "passage_row": passage_row, "suffix_len": suffix_len}


def reference(queries, suffix_keys, suffix_values, passage_keys, passage_values, cites, passage_row, suffix_len):
    groups = HQ // KVH
    prefix = CITE * PLEN
    positions = jnp.arange(SUF, dtype=jnp.int32)
    key_index = jnp.arange(prefix + SUF, dtype=jnp.int32)
    visible = (key_index[None, :] < prefix) | (key_index[None, :] - prefix <= positions[:, None])
    scale = HD ** -0.5

    def one_request(request):
        rows = passage_row[cites[request]]
        keys = jnp.concatenate([passage_keys[rows].reshape(prefix, KVH * HD), suffix_keys[request]], axis=0)
        values = jnp.concatenate([passage_values[rows].reshape(prefix, KVH * HD), suffix_values[request]], axis=0)
        query_heads = queries[request].reshape(SUF, KVH, groups, HD).transpose(1, 0, 2, 3)
        key_heads = keys.reshape(prefix + SUF, KVH, HD).transpose(1, 0, 2)
        value_heads = values.reshape(prefix + SUF, KVH, HD).transpose(1, 0, 2)

        def one_head(item):
            query_g, key_g, value_g = item
            scores = jnp.einsum("rgd,kd->rgk", query_g.astype(jnp.float32), key_g.astype(jnp.float32)) * scale
            scores = jnp.where(visible[:, None, :], scores, -1e30)
            peak = jnp.max(scores, axis=-1, keepdims=True)
            weights = jnp.exp(scores - peak)
            probs = (weights / jnp.sum(weights, axis=-1, keepdims=True)).astype(jnp.bfloat16)
            return jnp.einsum("rgk,kd->rgd", probs.astype(jnp.float32), value_g.astype(jnp.float32))

        output = lax.map(one_head, (query_heads, key_heads, value_heads))
        output = output.transpose(1, 0, 2, 3).reshape(SUF, HQ * HD)
        live = (positions < suffix_len[request])[:, None]
        context = (output * live).astype(jnp.bfloat16)
        dec_keys = jnp.where(live, suffix_keys[request], jnp.zeros_like(suffix_keys[request]))
        dec_values = jnp.where(live, suffix_values[request], jnp.zeros_like(suffix_values[request]))
        return context, dec_keys, dec_values

    context, decode_keys, decode_values = lax.map(one_request, jnp.arange(NREQ, dtype=jnp.int32))
    return context, decode_keys, decode_values
```

```python
import functools
import math

import jax
import jax.numpy as jnp
from jax import lax
from jax.experimental import pallas as pl
from jax.experimental.pallas import tpu as pltpu
from jax.sharding import PartitionSpec as P

HD = 128
STEP_KEYS = 1024
STACK = 4
FACTOR = HD ** (-0.5) * math.log2(math.e)


def flip(me, d, n):
    out, bit = 0, 1
    while bit < n:
        out = out + ((me // bit + d // bit) % 2) * bit
        bit *= 2
    return out


def pick_kernel(n, cite, rows_ref, rank_ref, pk_ref, pv_ref, out_ref, sem):
    column = pl.ds(pl.multiple_of(rank_ref[0] * HD, HD), HD)

    def copies(i):
        made = []
        for c in range(cite):
            row = rows_ref[i, c]
            for which, ref in enumerate((pk_ref, pv_ref)):
                made.append(
                    pltpu.make_async_copy(
                        ref.at[row, :, column], out_ref.at[i, which, c], sem.at[i, c, which]
                    )
                )
        return made

    @pl.loop(0, n)
    def _(i):
        for copy in copies(i):
            copy.start()

    @pl.loop(0, n)
    def _(i):
        for copy in copies(i):
            copy.wait()


def pick(rows, rank, passage_keys, passage_values):
    n, cite = rows.shape
    part = passage_keys.shape[1]
    return pl.pallas_call(
        functools.partial(pick_kernel, n, cite),
        out_shape=jax.ShapeDtypeStruct((n, 2, cite, part, HD), passage_keys.dtype),
        in_specs=[
            pl.BlockSpec(memory_space=pltpu.SMEM),
            pl.BlockSpec(memory_space=pltpu.SMEM),
            pl.BlockSpec(memory_space=pl.ANY),
            pl.BlockSpec(memory_space=pl.ANY),
        ],
        out_specs=pl.BlockSpec(memory_space=pl.ANY),
        scratch_shapes=[pltpu.SemaphoreType.DMA((n, cite, 2))],
        name="pick",
    )(rows, rank, passage_keys, passage_values)


def attend_kernel(
    n_store, n_tp, group, heads,
    q_ref, sk_ref, sv_ref, send_ref, ctx_ref, dk_ref, dv_ref,
    qbuf, kvbuf, skbuf, svbuf, obuf, acc, peak,
    kv_send, kv_recv, q_send, q_recv, s_send, s_recv, c_send, c_recv, own_sem,
):
    me = lax.axis_index("store")
    rank = lax.axis_index("tp")
    tok = q_ref.shape[0]
    width = heads * HD
    steps = n_store // group
    keys_in = kvbuf.shape[2]
    MESH = pl.DeviceIdType.MESH

    def columns(index, size):
        return pl.ds(pl.multiple_of(index * size, size), size)

    def kv_copy(d):
        return pltpu.make_async_remote_copy(
            src_ref=send_ref.at[d], dst_ref=kvbuf.at[d],
            send_sem=kv_send.at[d], recv_sem=kv_recv.at[d],
            device_id=(flip(me, d, n_store), rank), device_id_type=MESH,
        )

    def q_copy(d):
        other = flip(rank, d, n_tp)
        return pltpu.make_async_remote_copy(
            src_ref=q_ref.at[:, columns(other, width)], dst_ref=qbuf.at[d],
            send_sem=q_send.at[d], recv_sem=q_recv.at[d],
            device_id=(me, other), device_id_type=MESH,
        )

    def s_copies(d):
        other = flip(rank, d, n_tp)
        return [
            pltpu.make_async_remote_copy(
                src_ref=src.at[:, columns(other, HD)], dst_ref=dst.at[columns(rank, tok)],
                send_sem=s_send.at[w, d], recv_sem=s_recv.at[w, d],
                device_id=(me, other), device_id_type=MESH,
            )
            for w, (src, dst) in enumerate(((sk_ref, skbuf), (sv_ref, svbuf)))
        ]

    def s_arrivals(d):
        other = flip(rank, d, n_tp)
        return [
            pltpu.make_async_remote_copy(
                src_ref=src.at[:, columns(other, HD)], dst_ref=dst.at[columns(other, tok)],
                send_sem=s_send.at[w, d], recv_sem=s_recv.at[w, d],
                device_id=(me, other), device_id_type=MESH,
            )
            for w, (src, dst) in enumerate(((sk_ref, skbuf), (sv_ref, svbuf)))
        ]

    def c_copy(d):
        other = flip(rank, d, n_tp)
        return pltpu.make_async_remote_copy(
            src_ref=obuf.at[d], dst_ref=ctx_ref.at[:, columns(rank, width)],
            send_sem=c_send.at[d], recv_sem=c_recv.at[d],
            device_id=(me, other), device_id_type=MESH,
        )

    def c_arrival(d):
        other = flip(rank, d, n_tp)
        return pltpu.make_async_remote_copy(
            src_ref=obuf.at[d], dst_ref=ctx_ref.at[:, columns(other, width)],
            send_sem=c_send.at[d], recv_sem=c_recv.at[d],
            device_id=(me, other), device_id_type=MESH,
        )

    own = [
        pltpu.make_async_copy(q_ref.at[:, columns(rank, width)], qbuf.at[0], own_sem.at[0]),
        pltpu.make_async_copy(send_ref.at[0], kvbuf.at[0], own_sem.at[1]),
        pltpu.make_async_copy(sk_ref.at[:, columns(rank, HD)], skbuf.at[columns(rank, tok)], own_sem.at[2]),
        pltpu.make_async_copy(sv_ref.at[:, columns(rank, HD)], svbuf.at[columns(rank, tok)], own_sem.at[3]),
    ]
    for copy in own:
        copy.start()

    barrier = pltpu.get_barrier_semaphore()

    @pl.loop(1, n_store)
    def _(d):
        pl.semaphore_signal(barrier, inc=1, device_id=(flip(me, d, n_store), rank), device_id_type=MESH)

    for d in range(1, n_tp):
        pl.semaphore_signal(barrier, inc=1, device_id=(me, flip(rank, d, n_tp)), device_id_type=MESH)
    pl.semaphore_wait(barrier, n_store - 1 + n_tp - 1)

    for d in range(1, n_tp):
        q_copy(d).start()

    @pl.loop(1, n_store)
    def _(d):
        kv_copy(d).start()

    for d in range(1, n_tp):
        for copy in s_copies(d):
            copy.start()

    peak[...] = jnp.full_like(peak, -jnp.inf)
    acc[...] = jnp.zeros_like(acc)

    def unit(q, keys, values, hidden=None):
        count = keys.shape[0]
        wide = jnp.concatenate([values, jnp.ones_like(values)], axis=1)
        for first in range(0, heads, STACK):
            stacked = jnp.concatenate(
                [qbuf[q, :, h * HD:(h + 1) * HD] for h in range(first, first + STACK)], axis=0
            )
            scores = lax.dot_general(
                stacked, keys, (((1,), (1,)), ((), ())), preferred_element_type=jnp.float32
            )
            if hidden is not None:
                scores = jnp.where(hidden, -1e30, scores)
            rows = STACK * tok
            before = peak[q, first:first + STACK].reshape(rows, HD)
            now = jnp.maximum(before, jnp.max(scores, axis=1, keepdims=True))
            decay = jnp.exp2((before - now) * FACTOR)
            base = now * FACTOR
            weights = jnp.exp2(
                scores * FACTOR - jnp.concatenate([base] * (count // HD), axis=1)
            ).astype(jnp.bfloat16)
            part = jnp.dot(weights, wide, preferred_element_type=jnp.float32)
            held = acc[q, first:first + STACK].reshape(rows, 2 * HD)
            acc[q, first:first + STACK] = (
                held * jnp.concatenate([decay, decay], axis=1) + part
            ).reshape(STACK, tok, 2 * HD)
            peak[q, first:first + STACK] = now.reshape(STACK, tok, HD)

    def passage_unit(q, step):
        at = pl.ds(step * group, group)
        keys = kvbuf[at, 0].reshape(group * keys_in, HD)
        values = kvbuf[at, 1].reshape(group * keys_in, HD)
        unit(q, keys, values)

    def suffix_unit(q):
        total = n_tp * tok
        shape = (STACK * tok, total)
        position = flip(rank, q, n_tp) * tok + lax.broadcasted_iota(jnp.int32, shape, 0) % tok
        unit(q, skbuf[...], svbuf[...], lax.broadcasted_iota(jnp.int32, shape, 1) > position)

    def await_step(step):
        @pl.loop(0, group)
        def _(g):
            kv_copy(step * group + g).wait_recv()

    near = n_tp // 2
    own[0].wait()
    own[1].wait()

    @pl.loop(1, group)
    def _(d):
        kv_copy(d).wait_recv()

    @pl.loop(0, near)
    def _(q):
        @pl.when(q > 0)
        def _():
            q_copy(q).wait_recv()

        passage_unit(q, 0)

    @pl.loop(1, steps - 1)
    def _(step):
        await_step(step)

        @pl.loop(0, near)
        def _(q):
            passage_unit(q, step)

    @pl.loop(near, n_tp)
    def _(q):
        q_copy(q).wait_recv()

        @pl.loop(0, steps - 1)
        def _(step):
            passage_unit(q, step)

    own[2].wait()
    own[3].wait()
    for d in range(1, n_tp):
        for copy in s_arrivals(d):
            copy.wait_recv()
    dk_ref[...] = skbuf[...]
    dv_ref[...] = svbuf[...]

    @pl.loop(0, n_tp)
    def _(q):
        suffix_unit(q)

    await_step(steps - 1)

    @pl.loop(0, n_tp)
    def _(turn):
        q = n_tp - 1 - turn
        passage_unit(q, steps - 1)
        for h in range(heads):
            whole = acc[q, h]
            obuf[q, :, h * HD:(h + 1) * HD] = (whole[:, :HD] / whole[:, HD:]).astype(jnp.bfloat16)

        @pl.when(q > 0)
        def _():
            c_copy(q).start()

    last = pltpu.make_async_copy(obuf.at[0], ctx_ref.at[:, columns(rank, width)], own_sem.at[0])
    last.start()

    @pl.loop(1, n_store)
    def _(d):
        kv_copy(d).wait_send()

    for d in range(1, n_tp):
        q_copy(d).wait_send()
        for copy in s_copies(d):
            copy.wait_send()
        c_copy(d).wait_send()
        c_arrival(d).wait_recv()
    last.wait()


def attend(queries, suffix_keys, suffix_values, send):
    n_store, n_tp = lax.axis_size("store"), lax.axis_size("tp")
    tok, total = queries.shape
    heads = total // n_tp // HD
    keys_in = send.shape[2]
    group = min(n_store, max(1, STEP_KEYS // keys_in))
    dtype = queries.dtype
    dma = pltpu.SemaphoreType.DMA
    any_spec = pl.BlockSpec(memory_space=pl.ANY)
    vmem = pl.BlockSpec(memory_space=pltpu.VMEM)
    suffix = jax.ShapeDtypeStruct((n_tp * tok, HD), dtype)
    return pl.pallas_call(
        functools.partial(attend_kernel, n_store, n_tp, group, heads),
        out_shape=(jax.ShapeDtypeStruct(queries.shape, dtype), suffix, suffix),
        in_specs=[any_spec] * 4,
        out_specs=(any_spec, vmem, vmem),
        scratch_shapes=[
            pltpu.VMEM((n_tp, tok, heads * HD), dtype),
            pltpu.VMEM((n_store, 2, keys_in, HD), dtype),
            pltpu.VMEM((n_tp * tok, HD), dtype),
            pltpu.VMEM((n_tp * tok, HD), dtype),
            pltpu.VMEM((n_tp, tok, heads * HD), dtype),
            pltpu.VMEM((n_tp, heads, tok, 2 * HD), jnp.float32),
            pltpu.VMEM((n_tp, heads, tok, HD), jnp.float32),
            dma((n_store,)), dma((n_store,)),
            dma((n_tp,)), dma((n_tp,)),
            dma((2, n_tp)), dma((2, n_tp)),
            dma((n_tp,)), dma((n_tp,)),
            dma((4,)),
        ],
        compiler_params=pltpu.CompilerParams(
            collective_id=0, has_side_effects=True, vmem_limit_bytes=48 * 1024 * 1024
        ),
        name="attend",
    )(queries, suffix_keys, suffix_values, send)


def body(queries, suffix_keys, suffix_values, passage_keys, passage_values, cites, passage_row, suffix_len):
    n_store, n_tp = lax.axis_size("store"), lax.axis_size("tp")
    me, rank = lax.axis_index("store"), lax.axis_index("tp")
    tok = queries.shape[1]
    length = suffix_len[me]
    partners = flip(me, jnp.arange(n_store, dtype=jnp.int32), n_store)
    rows = passage_row[cites[partners]]
    send = pick(rows, jnp.full((1,), rank, jnp.int32), passage_keys, passage_values)
    cite, part = send.shape[2], send.shape[3]
    context, keys, values = attend(
        queries[0], suffix_keys[0], suffix_values[0], send.reshape(n_store, 2, cite * part, HD)
    )
    positions = rank * tok + jnp.arange(tok, dtype=jnp.int32)
    context = jnp.where((positions < length)[:, None], context, jnp.zeros_like(context))
    live = (jnp.arange(n_tp * tok, dtype=jnp.int32) < length)[:, None]
    keys = jnp.where(live, keys, jnp.zeros_like(keys))
    values = jnp.where(live, values, jnp.zeros_like(values))
    return context[None], keys[None], values[None]


def solution(mesh):
    in_specs = (
        P("store", "tp", None),
        P("store", "tp", None),
        P("store", "tp", None),
        P(None, "store", None),
        P(None, "store", None),
        P(),
        P(),
        P(),
    )
    out_specs = (P("store", "tp", None), P("store", None, "tp"), P("store", None, "tp"))
    return jax.shard_map(body, mesh=mesh, in_specs=in_specs, out_specs=out_specs, check_vma=False)
```

```python
import functools
import math

import jax
import jax.numpy as jnp
from jax import lax
from jax.experimental import pallas as pl
from jax.experimental.pallas import tpu as pltpu
from jax.sharding import PartitionSpec as P

HD = 128
STEP_KEYS = 1024
STACK = 4
FACTOR = HD ** (-0.5) * math.log2(math.e)


def flip(me, d, n):
    out, bit = 0, 1
    while bit < n:
        out = out + ((me // bit + d // bit) % 2) * bit
        bit *= 2
    return out


def pick_kernel(n, cite, rows_ref, rank_ref, pk_ref, pv_ref, out_ref, sem):
    column = pl.ds(pl.multiple_of(rank_ref[0] * HD, HD), HD)

    def copies(i):
        made = []
        for c in range(cite):
            row = rows_ref[i, c]
            for which, ref in enumerate((pk_ref, pv_ref)):
                made.append(
                    pltpu.make_async_copy(
                        ref.at[row, :, column], out_ref.at[i, which, c], sem.at[i, c, which]
                    )
                )
        return made

    @pl.loop(0, n)
    def _(i):
        for copy in copies(i):
            copy.start()

    @pl.loop(0, n)
    def _(i):
        for copy in copies(i):
            copy.wait()


def pick(rows, rank, passage_keys, passage_values):
    n, cite = rows.shape
    part = passage_keys.shape[1]
    return pl.pallas_call(
        functools.partial(pick_kernel, n, cite),
        out_shape=jax.ShapeDtypeStruct((n, 2, cite, part, HD), passage_keys.dtype),
        in_specs=[
            pl.BlockSpec(memory_space=pltpu.SMEM),
            pl.BlockSpec(memory_space=pltpu.SMEM),
            pl.BlockSpec(memory_space=pl.ANY),
            pl.BlockSpec(memory_space=pl.ANY),
        ],
        out_specs=pl.BlockSpec(memory_space=pltpu.VMEM),
        scratch_shapes=[pltpu.SemaphoreType.DMA((n, cite, 2))],
        name="pick",
    )(rows, rank, passage_keys, passage_values)


def attend_kernel(
    n_store, n_tp, group, heads,
    q_ref, sk_ref, sv_ref, send_ref, ctx_ref, dk_ref, dv_ref,
    qbuf, qwide, kvbuf, skbuf, svbuf, obuf, acc, peak,
    kv_send, kv_recv, q_send, q_recv, s_send, s_recv, c_send, c_recv, own_sem,
):
    me = lax.axis_index("store")
    rank = lax.axis_index("tp")
    tok = q_ref.shape[0]
    width = heads * HD
    steps = n_store // group
    keys_in = kvbuf.shape[2]
    MESH = pl.DeviceIdType.MESH

    def columns(index, size):
        return pl.ds(pl.multiple_of(index * size, size), size)

    def kv_copy(d):
        return pltpu.make_async_remote_copy(
            src_ref=send_ref.at[d], dst_ref=kvbuf.at[d],
            send_sem=kv_send.at[d], recv_sem=kv_recv.at[d],
            device_id=(flip(me, d, n_store), rank), device_id_type=MESH,
        )

    def q_copy(d):
        other = flip(rank, d, n_tp)
        return pltpu.make_async_remote_copy(
            src_ref=q_ref.at[:, columns(other, width)], dst_ref=qbuf.at[d],
            send_sem=q_send.at[d], recv_sem=q_recv.at[d],
            device_id=(me, other), device_id_type=MESH,
        )

    def s_copies(d):
        other = flip(rank, d, n_tp)
        return [
            pltpu.make_async_remote_copy(
                src_ref=src.at[:, columns(other, HD)], dst_ref=dst.at[columns(rank, tok)],
                send_sem=s_send.at[w, d], recv_sem=s_recv.at[w, d],
                device_id=(me, other), device_id_type=MESH,
            )
            for w, (src, dst) in enumerate(((sk_ref, skbuf), (sv_ref, svbuf)))
        ]

    def s_arrivals(d):
        other = flip(rank, d, n_tp)
        return [
            pltpu.make_async_remote_copy(
                src_ref=src.at[:, columns(other, HD)], dst_ref=dst.at[columns(other, tok)],
                send_sem=s_send.at[w, d], recv_sem=s_recv.at[w, d],
                device_id=(me, other), device_id_type=MESH,
            )
            for w, (src, dst) in enumerate(((sk_ref, skbuf), (sv_ref, svbuf)))
        ]

    def c_copy(d):
        other = flip(rank, d, n_tp)
        return pltpu.make_async_remote_copy(
            src_ref=obuf.at[d], dst_ref=ctx_ref.at[:, columns(rank, width)],
            send_sem=c_send.at[d], recv_sem=c_recv.at[d],
            device_id=(me, other), device_id_type=MESH,
        )

    def c_arrival(d):
        other = flip(rank, d, n_tp)
        return pltpu.make_async_remote_copy(
            src_ref=obuf.at[d], dst_ref=ctx_ref.at[:, columns(other, width)],
            send_sem=c_send.at[d], recv_sem=c_recv.at[d],
            device_id=(me, other), device_id_type=MESH,
        )

    own = [
        pltpu.make_async_copy(q_ref.at[:, columns(rank, width)], qbuf.at[0], own_sem.at[0]),
        pltpu.make_async_copy(send_ref.at[0], kvbuf.at[0], own_sem.at[1]),
        pltpu.make_async_copy(sk_ref.at[:, columns(rank, HD)], skbuf.at[columns(rank, tok)], own_sem.at[2]),
        pltpu.make_async_copy(sv_ref.at[:, columns(rank, HD)], svbuf.at[columns(rank, tok)], own_sem.at[3]),
    ]
    for copy in own:
        copy.start()

    barrier = pltpu.get_barrier_semaphore()

    @pl.loop(1, n_store)
    def _(d):
        pl.semaphore_signal(barrier, inc=1, device_id=(flip(me, d, n_store), rank), device_id_type=MESH)

    for d in range(1, n_tp):
        pl.semaphore_signal(barrier, inc=1, device_id=(me, flip(rank, d, n_tp)), device_id_type=MESH)
    pl.semaphore_wait(barrier, n_store - 1 + n_tp - 1)

    for d in [n_tp - 1, *range(1, n_tp - 1)]:
        q_copy(d).start()

    @pl.loop(1, n_store)
    def _(d):
        kv_copy(d).start()

    for d in range(1, n_tp):
        for copy in s_copies(d):
            copy.start()

    peak[...] = jnp.full_like(peak, -jnp.inf)
    acc[...] = jnp.zeros_like(acc)

    def unit(q, keys, values, hidden=None):
        count = keys.shape[0]
        wide = jnp.concatenate([values, jnp.ones_like(values)], axis=1)
        twice = jnp.concatenate([keys, keys], axis=1)
        for first in range(0, heads, STACK):
            stacked = qwide[q, first:first + STACK].reshape(STACK * tok, 2 * HD)
            scores = lax.dot_general(
                stacked, twice, (((1,), (1,)), ((), ())), preferred_element_type=jnp.float32
            )
            if hidden is not None:
                scores = jnp.where(hidden, -1e30, scores)
            rows = STACK * tok
            before = peak[q, first:first + STACK].reshape(rows, HD)
            now = jnp.maximum(before, jnp.max(scores, axis=1, keepdims=True))
            decay = jnp.exp2(before - now)
            weights = jnp.exp2(
                scores - jnp.concatenate([now] * (count // HD), axis=1)
            ).astype(jnp.bfloat16)
            part = jnp.dot(weights, wide, preferred_element_type=jnp.float32)
            held = acc[q, first:first + STACK].reshape(rows, 2 * HD)
            acc[q, first:first + STACK] = (
                held * jnp.concatenate([decay, decay], axis=1) + part
            ).reshape(STACK, tok, 2 * HD)
            peak[q, first:first + STACK] = now.reshape(STACK, tok, HD)

    def prepare(q):
        for h in range(heads):
            scaled = qbuf[q, :, h * HD:(h + 1) * HD].astype(jnp.float32) * FACTOR
            high = scaled.astype(jnp.bfloat16)
            low = (scaled - high.astype(jnp.float32)).astype(jnp.bfloat16)
            qwide[q, h] = jnp.concatenate([high, low], axis=1)

    def passage_unit(q, step):
        at = pl.ds(step * group, group)
        keys = kvbuf[at, 0].reshape(group * keys_in, HD)
        values = kvbuf[at, 1].reshape(group * keys_in, HD)
        unit(q, keys, values)

    def suffix_unit(q):
        total = n_tp * tok
        shape = (STACK * tok, total)
        position = flip(rank, q, n_tp) * tok + lax.broadcasted_iota(jnp.int32, shape, 0) % tok
        unit(q, skbuf[...], svbuf[...], lax.broadcasted_iota(jnp.int32, shape, 1) > position)

    def await_step(step):
        @pl.loop(0, group)
        def _(g):
            kv_copy(step * group + g).wait_recv()

    far = n_tp - 1
    own[0].wait()
    own[1].wait()

    @pl.loop(1, group)
    def _(d):
        kv_copy(d).wait_recv()

    @pl.loop(0, 2)
    def _(j):
        q = j * far

        @pl.when(j > 0)
        def _():
            q_copy(q).wait_recv()

        prepare(q)
        passage_unit(q, 0)

    @pl.loop(1, steps - 1)
    def _(step):
        await_step(step)

        @pl.loop(0, 2)
        def _(j):
            passage_unit(j * far, step)

    def catch_up(q):
        q_copy(q).wait_recv()
        prepare(q)

        @pl.loop(0, steps - 1)
        def _(step):
            passage_unit(q, step)

    catch_up(1)

    @pl.loop(0, n_tp)
    def _(turn):
        q = n_tp - 1 - turn

        @pl.when((q > 1) & (q < far))
        def _():
            catch_up(q)

        @pl.when(turn == 0)
        def _():
            own[2].wait()
            own[3].wait()
            for d in range(1, n_tp):
                for copy in s_arrivals(d):
                    copy.wait_recv()
            dk_ref[...] = skbuf[...]
            dv_ref[...] = svbuf[...]
            await_step(steps - 1)

        suffix_unit(q)
        passage_unit(q, steps - 1)
        for h in range(heads):
            whole = acc[q, h]
            obuf[q, :, h * HD:(h + 1) * HD] = (whole[:, :HD] / whole[:, HD:]).astype(jnp.bfloat16)

        @pl.when(q > 0)
        def _():
            c_copy(q).start()

    last = pltpu.make_async_copy(obuf.at[0], ctx_ref.at[:, columns(rank, width)], own_sem.at[0])
    last.start()

    @pl.loop(1, n_store)
    def _(d):
        kv_copy(d).wait_send()

    for d in range(1, n_tp):
        q_copy(d).wait_send()
        for copy in s_copies(d):
            copy.wait_send()
        c_copy(d).wait_send()
        c_arrival(d).wait_recv()
    last.wait()


def attend(queries, suffix_keys, suffix_values, send):
    n_store, n_tp = lax.axis_size("store"), lax.axis_size("tp")
    tok, total = queries.shape
    heads = total // n_tp // HD
    keys_in = send.shape[2]
    group = min(n_store, max(1, STEP_KEYS // keys_in))
    dtype = queries.dtype
    dma = pltpu.SemaphoreType.DMA
    any_spec = pl.BlockSpec(memory_space=pl.ANY)
    vmem = pl.BlockSpec(memory_space=pltpu.VMEM)
    suffix = jax.ShapeDtypeStruct((n_tp * tok, HD), dtype)
    return pl.pallas_call(
        functools.partial(attend_kernel, n_store, n_tp, group, heads),
        out_shape=(jax.ShapeDtypeStruct(queries.shape, dtype), suffix, suffix),
        in_specs=[any_spec] * 4,
        out_specs=(any_spec, vmem, vmem),
        scratch_shapes=[
            pltpu.VMEM((n_tp, tok, heads * HD), dtype),
            pltpu.VMEM((n_tp, heads, tok, 2 * HD), dtype),
            pltpu.VMEM((n_store, 2, keys_in, HD), dtype),
            pltpu.VMEM((n_tp * tok, HD), dtype),
            pltpu.VMEM((n_tp * tok, HD), dtype),
            pltpu.VMEM((n_tp, tok, heads * HD), dtype),
            pltpu.VMEM((n_tp, heads, tok, 2 * HD), jnp.float32),
            pltpu.VMEM((n_tp, heads, tok, HD), jnp.float32),
            dma((n_store,)), dma((n_store,)),
            dma((n_tp,)), dma((n_tp,)),
            dma((2, n_tp)), dma((2, n_tp)),
            dma((n_tp,)), dma((n_tp,)),
            dma((4,)),
        ],
        compiler_params=pltpu.CompilerParams(
            collective_id=0, has_side_effects=True, vmem_limit_bytes=48 * 1024 * 1024
        ),
        name="attend",
    )(queries, suffix_keys, suffix_values, send)


def body(queries, suffix_keys, suffix_values, passage_keys, passage_values, cites, passage_row, suffix_len):
    n_store, n_tp = lax.axis_size("store"), lax.axis_size("tp")
    me, rank = lax.axis_index("store"), lax.axis_index("tp")
    tok = queries.shape[1]
    length = suffix_len[me]
    partners = flip(me, jnp.arange(n_store, dtype=jnp.int32), n_store)
    rows = passage_row[cites[partners]]
    send = pick(rows, jnp.full((1,), rank, jnp.int32), passage_keys, passage_values)
    cite, part = send.shape[2], send.shape[3]
    context, keys, values = attend(
        queries[0], suffix_keys[0], suffix_values[0], send.reshape(n_store, 2, cite * part, HD)
    )
    positions = rank * tok + jnp.arange(tok, dtype=jnp.int32)
    context = jnp.where((positions < length)[:, None], context, jnp.zeros_like(context))
    live = (jnp.arange(n_tp * tok, dtype=jnp.int32) < length)[:, None]
    keys = jnp.where(live, keys, jnp.zeros_like(keys))
    values = jnp.where(live, values, jnp.zeros_like(values))
    return context[None], keys[None], values[None]


def solution(mesh):
    in_specs = (
        P("store", "tp", None),
        P("store", "tp", None),
        P("store", "tp", None),
        P(None, "store", None),
        P(None, "store", None),
        P(),
        P(),
        P(),
    )
    out_specs = (P("store", "tp", None), P("store", None, "tp"), P("store", None, "tp"))
    return jax.shard_map(body, mesh=mesh, in_specs=in_specs, out_specs=out_specs, check_vma=False)
```
